1024 devices in a mesh: fsdp: 64 (over z, y), rep: 16 (over x, core).
Axes of the slice: x: 8, y: 8, z: 8, core: 2. Of those that a mesh axis runs over, the one named last changes fastest.
Arguments:
- grad_parts: bfloat16 [16, 4096, 16, 256], P('rep', 'fsdp'), may hold values from -0.3125 to 0.3125
- slot_block: int32 [64, 2], replicated, may hold values from -1 to 63, as said below
- stat_left: float32 [64, 2, 1024, 1024], P('fsdp', None, 'rep'), as said below
- stat_right: float32 [64, 2, 1024, 1024], P('fsdp', None, 'rep'), as said below
- root_left: bfloat16 [64, 2, 1024, 1024], P('fsdp'), as said below
- root_right: bfloat16 [64, 2, 1024, 1024], P('fsdp', None, None, 'rep'), as said below
Outputs:
- new_left: float32 [64, 2, 1024, 1024], P('fsdp', None, 'rep')
- new_right: float32 [64, 2, 1024, 1024], P('fsdp', None, 'rep')
- precond: bfloat16 [4096, 16, 1024], P('fsdp', None, 'rep')
The draws below stay inside these ranges and needn't reach their ends.
Inputs may be any that keep to these rules, and one draw needn't show every extreme that they name: `slot_block`: every block number 0 to 63 stands in exactly one slot; all other slots hold -1; no owner holds more than 1 block of one band (blocks a * 16 to (a + 1) * 16 - 1), and some owner holds exactly 1 of some band; in every draw some owner has all 2 slots filled, and loads differ between owners. `stat_left`: Symmetric. `stat_right`: Symmetric. `root_left`: Symmetric. `root_right`: Symmetric.
All inputs are finite; a program needn't handle non-finite values.
Results may differ from the reference program's by a relative error of at most 0.015.
Values may be sent and summed in bfloat16 or wider, within the bound.
No kernel may reach another device: no remote copies, remote signals or barrier semaphores. Data moves between devices by JAX's collectives and lax.ppermute only.
A program may use at most 64 MiB of HBM per device.

```python
import math
import jax
import jax.numpy as jnp
from jax import lax

BLOCK = 1024
ROWS = 4096
REPLICAS = 4
SPLIT = 4
PIECE = 256
NCB = 16
NBANDS = 4
NBLK = 64
OWNERS = 64
MOST = 2
N_REP = 16


def symmetric_draw(key, diag_low, diag_high, noise_scale):
    normal_key, diagonal_key = jax.random.split(key)
    raw_normal = jax.random.normal(normal_key, (OWNERS, MOST, BLOCK, BLOCK), jnp.float32)
    symmetric = (raw_normal + jnp.swapaxes(raw_normal, -1, -2)) * (noise_scale * (0.5 / BLOCK) ** 0.5)
    log_diag = jax.random.uniform(diagonal_key, (OWNERS, MOST, BLOCK), jnp.float32, math.log(diag_low), math.log(diag_high))
    identity = jnp.eye(BLOCK, dtype=jnp.float32)
    return symmetric * (1.0 - identity) + jnp.exp(log_diag)[..., None] * identity


def draw_stat_left(key, part):
    key = jax.random.fold_in(key, 11)
    return symmetric_draw(key, 0.25, 2.0, 0.5)


def draw_stat_right(key, part):
    key = jax.random.fold_in(key, 12)
    return symmetric_draw(key, 0.25, 2.0, 0.5)


def draw_root_left(key, part):
    key = jax.random.fold_in(key, 13)
    return symmetric_draw(key, 1.0, 8.0, 1.2).astype(jnp.bfloat16)


def draw_root_right(key, part):
    key = jax.random.fold_in(key, 14)
    return symmetric_draw(key, 1.0, 8.0, 1.2).astype(jnp.bfloat16)


def draw_slot_block(key, part):
    key = jax.random.fold_in(key, 15)
    heavy_key, owner_key, order_key, column_key = jax.random.split(key, 4)
    ticket_total = OWNERS * MOST
    group_size = ticket_total // NBANDS
    heavy_owner = jax.random.randint(heavy_key, (), 0, OWNERS)
    owner_rank = jax.random.permutation(owner_key, OWNERS).astype(jnp.int32)
    slot_ids = jnp.arange(ticket_total, dtype=jnp.int32)
    owner_of = slot_ids // MOST
    within = slot_ids % MOST
    band_tag = (within + jnp.take(owner_rank, owner_of)) % NBANDS
    shuffled = jax.random.permutation(order_key, ticket_total).astype(jnp.int32)
    priority = jnp.where(owner_of == heavy_owner, within, ticket_total + shuffled)
    composite = band_tag * (2 * ticket_total) + priority
    ranked = jnp.argsort(composite)
    position = jnp.zeros((ticket_total,), jnp.int32).at[ranked].set(slot_ids)
    rank_in_band = position - band_tag * group_size
    chosen = rank_in_band < NCB
    column_order = jax.random.permutation(column_key, NCB).astype(jnp.int32)
    safe_rank = jnp.clip(rank_in_band, 0, NCB - 1)
    block_number = band_tag * NCB + jnp.take(column_order, safe_rank)
    filled_table = jnp.where(chosen, block_number, -1).astype(jnp.int32)
    return filled_table.reshape(OWNERS, MOST)


def raised(array, own_key, source, target, blocks, factor):
    owner, partner = [(jnp.arange(array.shape[dim]) // (array.shape[dim] // blocks)).reshape([-1 if axis == dim else 1 for axis in range(array.ndim)]) for dim in (source, target)]
    chosen = jax.random.permutation(own_key, blocks)[partner]
    strong = (owner == chosen) | (owner == (partner + blocks // 2) % blocks)
    return jnp.where(strong, factor * array, array)


def block_levels(own_key, shape, shards, low, largest):
    gain, own = 1.0, jax.random.fold_in(own_key, 6)
    for dim, shards_of in shards:
        heights = jnp.exp(jax.random.uniform(jax.random.fold_in(own, dim), (shards_of,), jnp.float32, low / len(shards), largest / len(shards)))
        gain = gain * jnp.repeat(heights, shape[dim] // shards_of).reshape([-1 if axis == dim else 1 for axis in range(len(shape))])
    return gain


def bell_draw_with(stream_key, extent, deviation, limit, cuts, heavy, kind=jnp.bfloat16):
    drawn = deviation * jax.random.normal(stream_key, extent, jnp.float32)
    if cuts:
        drawn = drawn * block_levels(stream_key, extent, cuts, -0.22, 0.18)
    return jnp.clip(raised(drawn, jax.random.fold_in(stream_key, 3), *heavy), -limit, limit).astype(kind)


def setup_inputs(seed: int = 0) -> dict:
    key_of = jax.random.split(jax.random.key(seed), 7)
    grad_parts = bell_draw_with(key_of[0], (N_REP, ROWS, NCB, PIECE), ((BLOCK * REPLICAS) ** -0.5), 0.3125, ((0, 16), (1, 64)), (0, 3, 16, 2.0))
    slot_block = draw_slot_block(jax.random.fold_in(key_of[6], 71), 0)
    stat_left = draw_stat_left(jax.random.fold_in(key_of[6], 71), 0)
    stat_right = draw_stat_right(jax.random.fold_in(key_of[6], 71), 0)
    root_left = draw_root_left(jax.random.fold_in(key_of[6], 71), 0)
    root_right = draw_root_right(jax.random.fold_in(key_of[6], 71), 0)
    return {"grad_parts": grad_parts, "slot_block": slot_block, "stat_left": stat_left, "stat_right": stat_right, "root_left": root_left, "root_right": root_right}


STAT_DECAY = 0.9


def owner_work(operands):
    slot_grads, left_stat, right_stat, left_root, right_root = operands
    widened = slot_grads.astype(jnp.float32)
    highest = lax.Precision.HIGHEST
    outer_left = jnp.einsum('mik,mjk->mij', widened, widened, precision=highest)
    outer_right = jnp.einsum('mki,mkj->mij', widened, widened, precision=highest)
    new_left = STAT_DECAY * left_stat + (1.0 - STAT_DECAY) * outer_left
    new_right = STAT_DECAY * right_stat + (1.0 - STAT_DECAY) * outer_right
    middle = jnp.einsum('mik,mkj->mij', widened, right_root.astype(jnp.float32), precision=highest).astype(jnp.bfloat16)
    result = jnp.einsum('mik,mkj->mij', left_root.astype(jnp.float32), middle.astype(jnp.float32), precision=highest).astype(jnp.bfloat16)
    return new_left, new_right, result


def reference(grad_parts, slot_block, stat_left, stat_right, root_left, root_right):
    grouped = grad_parts.astype(jnp.float32).reshape(SPLIT, REPLICAS, ROWS, NCB, PIECE)
    summed = jnp.sum(grouped, axis=1)
    summed = jnp.transpose(summed, (1, 2, 0, 3)).reshape(ROWS, NCB, BLOCK)
    gradient = summed.astype(jnp.bfloat16)
    blocks = gradient.reshape(NBANDS, BLOCK, NCB, BLOCK).transpose(0, 2, 1, 3).reshape(NBLK, BLOCK, BLOCK)
    flat_slots = slot_block.reshape(-1).astype(jnp.int32)
    occupied = flat_slots >= 0
    safe_index = jnp.where(occupied, flat_slots, 0).astype(jnp.int32)
    picked = jnp.take(blocks, safe_index, axis=0)
    picked = jnp.where(occupied[:, None, None], picked, jnp.zeros_like(picked))
    picked = picked.reshape(OWNERS, MOST, BLOCK, BLOCK)
    new_left, new_right, precond_blocks = lax.map(owner_work, (picked, stat_left, stat_right, root_left, root_right))
    target_slot = jnp.where(occupied, flat_slots, NBLK).astype(jnp.int32)
    placed = jnp.zeros((NBLK + 1, BLOCK, BLOCK), precond_blocks.dtype)
    placed = placed.at[target_slot].set(precond_blocks.reshape(OWNERS * MOST, BLOCK, BLOCK))[:NBLK]
    precond = placed.reshape(NBANDS, NCB, BLOCK, BLOCK).transpose(0, 2, 1, 3).reshape(ROWS, NCB, BLOCK)
    return new_left, new_right, precond
```

```python
import jax
import jax.numpy as jnp
from jax import lax
from jax.sharding import PartitionSpec as P

STAT_DECAY = 0.9


def exchanged(value, mask):
    size = lax.axis_size("rep")
    return lax.ppermute(value, "rep", [(r, r ^ mask) for r in range(size)])


def passed(value, step):
    size = lax.axis_size("rep")
    return lax.ppermute(value, "rep", [(r, (r + step) % size) for r in range(size)])


def taken(value, index):
    return lax.dynamic_index_in_dim(value, index, 0, keepdims=False)


def either(first, own, other):
    return jnp.where(first, own, other), jnp.where(first, other, own)


def local(grad_parts, slot_block, stat_left, stat_right, root_left, root_right):
    bf16, f32 = jnp.bfloat16, jnp.float32
    shard_rows, col_blocks = grad_parts.shape[1:3]
    block = stat_left.shape[3]
    owners, slot_count = slot_block.shape
    slab = root_right.shape[3]
    wide = 2 * slab
    chips = block // wide
    sources = block // shard_rows
    bands = owners // sources
    half = shard_rows // 2
    shard = lax.axis_index("fsdp")
    member = lax.axis_index("rep")
    core, chip = member % 2, member // 2
    first = core == 0
    my_band = shard // sources

    block_column = slot_block - my_band * col_blocks
    in_band = (slot_block >= 0) & (block_column >= 0) & (block_column < col_blocks)
    sends = jnp.any(
        in_band[:, :, None] & (block_column[:, :, None] == jnp.arange(col_blocks)), axis=1
    )
    owner_of = jnp.argmax(sends, axis=0)
    held = taken(slot_block, shard)
    occupied = held >= 0
    held_band = jnp.where(occupied, held // col_blocks, 0)
    own_occupied, other_occupied = taken(occupied, core), taken(occupied, 1 - core)
    own_band, other_band = taken(held_band, core), taken(held_band, 1 - core)

    partial = grad_parts[0]
    kept = lax.dynamic_slice_in_dim(partial, core * half, half, 0)
    given = lax.dynamic_slice_in_dim(partial, (1 - core) * half, half, 0)
    pair = kept.astype(f32) + exchanged(given, 1).astype(f32)
    side = chip % 2
    kept = lax.dynamic_slice_in_dim(pair, side * wide, wide, 2)
    given = lax.dynamic_slice_in_dim(pair, (1 - side) * wide, wide, 2)
    gradient = (kept + exchanged(given.astype(bf16), 2).astype(f32)).astype(bf16)

    outgoing = jnp.einsum(
        "oc,rcj->orj", sends.astype(bf16), gradient, preferred_element_type=f32
    ).astype(bf16)
    arrived = lax.all_to_all(outgoing, "fsdp", split_axis=0, concat_axis=0, tiled=True)
    banded = arrived.reshape(bands, sources, half, wide)
    own = jnp.where(own_occupied, taken(banded, own_band), 0)
    other = jnp.where(other_occupied, taken(banded, other_band), 0)

    upper, lower = either(first, own, exchanged(other, 1))
    piece = jnp.stack([upper, lower], axis=1).reshape(block, wide)
    right_pair = either(
        first, taken(root_right[0], core), exchanged(taken(root_right[0], 1 - core), 1)
    )
    right = jnp.concatenate(right_pair, axis=1)
    right = lax.dynamic_slice_in_dim(
        jnp.concatenate([right, right], axis=0), chip * wide, block, 0
    )
    left = taken(root_left[0], core)

    up, down = [piece], [piece]
    for _ in range(chips // 2 - 1):
        up.append(passed(up[-1], 2))
        down.append(passed(down[-1], -2))
    far = jnp.concatenate(
        [passed(up[-1][: block // 2], 2), passed(down[-1][block // 2 :], -2)], axis=0
    )
    whole = jnp.concatenate(down + [far] + up[:0:-1], axis=1)

    middle = jnp.dot(whole, right, preferred_element_type=f32).astype(bf16)
    result = jnp.dot(left, middle, preferred_element_type=f32).astype(bf16)

    parted = result.reshape(sources, 2, half, 2, slab)
    folded = [
        jnp.concatenate([parted[:, 0, :, k], parted[:, 1, :, k]], axis=-1) for k in range(2)
    ]
    own, given = either(first, *folded)
    other = exchanged(given, 1)
    band_ids = jnp.arange(bands)[:, None, None, None]
    returning = jnp.where(
        own_occupied & (band_ids == own_band),
        own[None],
        jnp.where(other_occupied & (band_ids == other_band), other[None], 0),
    ).reshape(owners, half, wide)
    came_back = lax.all_to_all(returning, "fsdp", split_axis=0, concat_axis=0, tiled=True)
    picked = jnp.take(came_back, owner_of, axis=0)
    precond = jnp.concatenate([picked[:, :, :slab], picked[:, :, slab:]], axis=1)
    precond = precond.transpose(1, 0, 2)

    rows = lax.dynamic_slice_in_dim(whole, chip * wide, wide, 0)
    left_rows = jnp.einsum("ic,kc->ik", rows, whole, preferred_element_type=f32)
    right_rows = jnp.einsum("ki,kc->ic", piece, whole, preferred_element_type=f32)
    right_rows = lax.dynamic_slice_in_dim(
        jnp.concatenate([right_rows, right_rows], axis=1),
        (chips - chip) % chips * wide,
        block,
        1,
    )
    both = jnp.stack([left_rows, right_rows])
    own = lax.dynamic_slice_in_dim(both, core * slab, slab, 1)
    other = exchanged(lax.dynamic_slice_in_dim(both, (1 - core) * slab, slab, 1), 1)
    products = jnp.stack(either(first, own, other), axis=1)
    new_left = STAT_DECAY * stat_left[0] + (1.0 - STAT_DECAY) * products[0]
    new_right = STAT_DECAY * stat_right[0] + (1.0 - STAT_DECAY) * products[1]
    return (new_left[None], new_right[None], precond)


def solution(mesh):
    placed = (
        P("rep", "fsdp", None, None),
        P(),
        P("fsdp", None, "rep", None),
        P("fsdp", None, "rep", None),
        P("fsdp", None, None, None),
        P("fsdp", None, None, "rep"),
    )
    return jax.shard_map(
        local,
        mesh=mesh,
        in_specs=placed,
        out_specs=(
            P("fsdp", None, "rep", None),
            P("fsdp", None, "rep", None),
            P("fsdp", None, "rep"),
        ),
        check_vma=False,
    )
```

```python
import jax
import jax.numpy as jnp
from jax import lax
from jax.sharding import PartitionSpec as P

STAT_DECAY = 0.9


def taken(value, index):
    return lax.dynamic_index_in_dim(value, index, 0, keepdims=False)


def either(first, own, other):
    return jnp.where(first, own, other), jnp.where(first, other, own)


def over_core(value):
    size = lax.axis_size("rep")
    return lax.ppermute(value, "rep", [(r, r ^ 1) for r in range(size)])


def same_core():
    size = lax.axis_size("rep")
    return [list(range(c, size, 2)) for c in range(2)]


def over_chips(value):
    return lax.all_to_all(
        value, "rep", split_axis=0, concat_axis=0, axis_index_groups=same_core(), tiled=True
    )


def local(grad_parts, slot_block, stat_left, stat_right, root_left, root_right):
    bf16, f32 = jnp.bfloat16, jnp.float32
    shard_rows, col_blocks, piece = grad_parts.shape[1:]
    block = stat_left.shape[3]
    owners, slot_count = slot_block.shape
    slab = root_right.shape[3]
    wide = 2 * slab
    chips = block // wide
    pieces = block // piece
    sources = block // shard_rows
    bands = owners // sources
    half = shard_rows // 2
    few = shard_rows // chips
    shard = lax.axis_index("fsdp")
    member = lax.axis_index("rep")
    core, chip = member % 2, member // 2
    first = core == 0
    my_band = shard // sources

    block_column = slot_block - my_band * col_blocks
    in_band = (slot_block >= 0) & (block_column >= 0) & (block_column < col_blocks)
    sends = jnp.any(
        in_band[:, :, None] & (block_column[:, :, None] == jnp.arange(col_blocks)), axis=1
    )
    owner_of = jnp.argmax(sends, axis=0)
    held = taken(slot_block, shard)
    occupied = held >= 0
    held_band = jnp.where(occupied, held // col_blocks, 0)
    own_occupied, other_occupied = taken(occupied, core), taken(occupied, 1 - core)
    own_band, other_band = taken(held_band, core), taken(held_band, 1 - core)

    columns = jnp.swapaxes(root_right[0], 1, 2)
    right = taken(lax.all_gather(columns, "rep", axis=1, tiled=True), core)

    partial = grad_parts[0]
    kept = lax.dynamic_slice_in_dim(partial, core * wide, wide, 2)
    given = lax.dynamic_slice_in_dim(partial, (1 - core) * wide, wide, 2)
    pair = (kept.astype(f32) + over_core(given).astype(f32)).astype(bf16)
    spread = over_chips(pair).reshape(pieces, chips // pieces, few, col_blocks, wide)
    summed = jnp.sum(spread.astype(f32), axis=1).astype(bf16)

    outgoing = jnp.einsum(
        "oc,prcj->oprj", sends.astype(bf16), summed, preferred_element_type=f32
    ).astype(bf16)
    outgoing = outgoing.reshape(owners, pieces * few, wide)
    arrived = lax.all_to_all(outgoing, "fsdp", split_axis=0, concat_axis=0, tiled=True)
    arrived, right = lax.optimization_barrier((arrived, right))
    banded = arrived.reshape(bands, sources, pieces, few, wide)
    own = jnp.where(own_occupied, taken(banded, own_band), 0)
    other = jnp.where(other_occupied, taken(banded, other_band), 0)
    rows = jnp.stack(either(first, own, over_core(other)), axis=2)
    rows = rows.transpose(0, 3, 1, 2, 4).reshape(sources, few, block)

    whole = lax.all_gather(
        rows, "rep", axis=1, tiled=True, axis_index_groups=same_core()
    ).reshape(block, block)

    middle = jnp.dot(
        rows.reshape(-1, block), right, preferred_element_type=f32
    ).astype(bf16)
    turned = middle.reshape(sources * few, chips, wide).transpose(1, 0, 2)
    columns = over_chips(turned).reshape(chips, sources, few, wide)
    columns = columns.transpose(1, 0, 2, 3).reshape(block, wide)
    result = jnp.dot(
        taken(root_left[0], core), columns, preferred_element_type=f32
    ).astype(bf16)

    parted = result.reshape(sources, 2, half, 2, slab)
    folded = [
        jnp.concatenate([parted[:, 0, :, k], parted[:, 1, :, k]], axis=-1) for k in range(2)
    ]
    own, given = either(first, *folded)
    other = over_core(given)
    band_ids = jnp.arange(bands)[:, None, None, None]
    returning = jnp.where(
        own_occupied & (band_ids == own_band),
        own[None],
        jnp.where(other_occupied & (band_ids == other_band), other[None], 0),
    ).reshape(owners, half, wide)
    came_back = lax.all_to_all(returning, "fsdp", split_axis=0, concat_axis=0, tiled=True)
    picked = jnp.take(came_back, owner_of, axis=0)
    precond = jnp.concatenate([picked[:, :, :slab], picked[:, :, slab:]], axis=1)
    precond = precond.transpose(1, 0, 2)

    mine = lax.dynamic_slice_in_dim(whole, chip * wide, wide, 0)
    left_rows = jnp.einsum("ic,kc->ik", mine, whole, preferred_element_type=f32)
    mine = lax.dynamic_slice_in_dim(whole, chip * wide, wide, 1)
    right_rows = jnp.einsum("ki,kc->ic", mine, whole, preferred_element_type=f32)
    both = jnp.stack([left_rows, right_rows])
    own = lax.dynamic_slice_in_dim(both, core * slab, slab, 1)
    other = over_core(lax.dynamic_slice_in_dim(both, (1 - core) * slab, slab, 1))
    products = jnp.stack(either(first, own, other), axis=1)
    new_left = STAT_DECAY * stat_left[0] + (1.0 - STAT_DECAY) * products[0]
    new_right = STAT_DECAY * stat_right[0] + (1.0 - STAT_DECAY) * products[1]
    return (new_left[None], new_right[None], precond)


def solution(mesh):
    placed = (
        P("rep", "fsdp", None, None),
        P(),
        P("fsdp", None, "rep", None),
        P("fsdp", None, "rep", None),
        P("fsdp", None, None, None),
        P("fsdp", None, None, "rep"),
    )
    return jax.shard_map(
        local,
        mesh=mesh,
        in_specs=placed,
        out_specs=(
            P("fsdp", None, "rep", None),
            P("fsdp", None, "rep", None),
            P("fsdp", None, "rep"),
        ),
        check_vma=False,
    )
```

```python
import jax
import jax.numpy as jnp
from jax import lax
from jax.sharding import PartitionSpec as P

STAT_DECAY = 0.9


def over_core(value):
    size = lax.axis_size("rep")
    both = lax.all_gather(
        value, "rep", axis_index_groups=[[r, r + 1] for r in range(0, size, 2)]
    )
    return taken(both, 1 - lax.axis_index("rep") % 2)


def exchanged(value, mask):
    size = lax.axis_size("rep")
    return lax.ppermute(value, "rep", [(r, r ^ mask) for r in range(size)])


def passed(value, step):
    size = lax.axis_size("rep")
    return lax.ppermute(value, "rep", [(r, (r + step) % size) for r in range(size)])


def taken(value, index):
    return lax.dynamic_index_in_dim(value, index, 0, keepdims=False)


def either(first, own, other):
    return jnp.where(first, own, other), jnp.where(first, other, own)


def local(grad_parts, slot_block, stat_left, stat_right, root_left, root_right):
    bf16, f32 = jnp.bfloat16, jnp.float32
    shard_rows, col_blocks = grad_parts.shape[1:3]
    block = stat_left.shape[3]
    owners, slot_count = slot_block.shape
    slab = root_right.shape[3]
    wide = 2 * slab
    chips = block // wide
    sources = block // shard_rows
    bands = owners // sources
    half = shard_rows // 2
    shard = lax.axis_index("fsdp")
    member = lax.axis_index("rep")
    core, chip = member % 2, member // 2
    first = core == 0
    my_band = shard // sources

    block_column = slot_block - my_band * col_blocks
    in_band = (slot_block >= 0) & (block_column >= 0) & (block_column < col_blocks)
    sends = jnp.any(
        in_band[:, :, None] & (block_column[:, :, None] == jnp.arange(col_blocks)), axis=1
    )
    owner_of = jnp.argmax(sends, axis=0)
    held = taken(slot_block, shard)
    occupied = held >= 0
    held_band = jnp.where(occupied, held // col_blocks, 0)
    own_occupied, other_occupied = taken(occupied, core), taken(occupied, 1 - core)
    own_band, other_band = taken(held_band, core), taken(held_band, 1 - core)

    partial = grad_parts[0]
    kept = lax.dynamic_slice_in_dim(partial, core * half, half, 0)
    given = lax.dynamic_slice_in_dim(partial, (1 - core) * half, half, 0)
    pair = kept.astype(f32) + over_core(given).astype(f32)
    side = chip % 2
    kept = lax.dynamic_slice_in_dim(pair, side * wide, wide, 2)
    given = lax.dynamic_slice_in_dim(pair, (1 - side) * wide, wide, 2)
    gradient = (kept + exchanged(given.astype(bf16), 2).astype(f32)).astype(bf16)

    outgoing = jnp.einsum(
        "oc,rcj->orj", sends.astype(bf16), gradient, preferred_element_type=f32
    ).astype(bf16)
    arrived = lax.all_to_all(outgoing, "fsdp", split_axis=0, concat_axis=0, tiled=True)
    blank = jnp.zeros((owners, half, wide), bf16)
    arrived, blank = lax.optimization_barrier((arrived, blank))
    banded = arrived.reshape(bands, sources, half, wide)
    own = jnp.where(own_occupied, taken(banded, own_band), 0)
    other = jnp.where(other_occupied, taken(banded, other_band), 0)

    upper, lower = either(first, own, over_core(other))
    piece = jnp.stack([upper, lower], axis=1).reshape(block, wide)
    right_pair = either(
        first, taken(root_right[0], core), over_core(taken(root_right[0], 1 - core))
    )
    right = jnp.concatenate(right_pair, axis=1)
    right = lax.dynamic_slice_in_dim(
        jnp.concatenate([right, right], axis=0), chip * wide, block, 0
    )
    left = taken(root_left[0], core)

    up, down = [piece], [piece]
    for _ in range(chips // 2 - 1):
        up.append(passed(up[-1], 2))
        down.append(passed(down[-1], -2))
    far = jnp.concatenate(
        [passed(up[-1][: block // 2], 2), passed(down[-1][block // 2 :], -2)], axis=0
    )
    slabs = down + [far] + up[:0:-1]
    parts = [
        jnp.dot(slabs[d], right[d * wide : (d + 1) * wide], preferred_element_type=f32)
        for d in range(chips)
    ]
    near = parts[0] + ((parts[1] + parts[-1]) + (parts[2] + parts[-2]))
    near = near + (parts[3] + parts[-3])
    middle = (near + parts[4]).astype(bf16)
    result = jnp.dot(left, middle, preferred_element_type=f32).astype(bf16)

    parted = result.reshape(sources, 2, half, 2, slab)
    folded = [
        jnp.concatenate([parted[:, 0, :, k], parted[:, 1, :, k]], axis=-1) for k in range(2)
    ]
    own, given = either(first, *folded)
    own_place = jnp.where(own_occupied, own_band, (other_band + 1) % bands)
    other_place = jnp.where(other_occupied, other_band, (own_band + 1) % bands)
    other = over_core(given)
    returning = blank.reshape(bands, sources, half, wide)
    returning = lax.dynamic_update_index_in_dim(
        returning, jnp.where(own_occupied, own, 0), own_place, 0
    )
    returning = lax.dynamic_update_index_in_dim(
        returning, jnp.where(other_occupied, other, 0), other_place, 0
    )
    returning = returning.reshape(owners, half, wide)
    *slabs, returning = lax.optimization_barrier((*slabs, returning))
    came_back = lax.all_to_all(returning, "fsdp", split_axis=0, concat_axis=0, tiled=True)
    picked = jnp.take(came_back, owner_of, axis=0)
    precond = jnp.concatenate([picked[:, :, :slab], picked[:, :, slab:]], axis=1)
    precond = precond.transpose(1, 0, 2)

    piece = slabs[0]
    whole = jnp.concatenate(slabs, axis=1)
    rows = lax.dynamic_slice_in_dim(whole, chip * wide, wide, 0)
    left_rows = jnp.einsum("ic,kc->ik", rows, whole, preferred_element_type=f32)
    right_rows = jnp.einsum("ki,kc->ic", piece, whole, preferred_element_type=f32)
    right_rows = lax.dynamic_slice_in_dim(
        jnp.concatenate([right_rows, right_rows], axis=1),
        (chips - chip) % chips * wide,
        block,
        1,
    )
    both = jnp.stack([left_rows, right_rows])
    own = lax.dynamic_slice_in_dim(both, core * slab, slab, 1)
    other = exchanged(lax.dynamic_slice_in_dim(both, (1 - core) * slab, slab, 1), 1)
    products = jnp.stack(either(first, own, other), axis=1)
    new_left = STAT_DECAY * stat_left[0] + (1.0 - STAT_DECAY) * products[0]
    new_right = STAT_DECAY * stat_right[0] + (1.0 - STAT_DECAY) * products[1]
    return (new_left[None], new_right[None], precond)


def solution(mesh):
    placed = (
        P("rep", "fsdp", None, None),
        P(),
        P("fsdp", None, "rep", None),
        P("fsdp", None, "rep", None),
        P("fsdp", None, None, None),
        P("fsdp", None, None, "rep"),
    )
    return jax.shard_map(
        local,
        mesh=mesh,
        in_specs=placed,
        out_specs=(
            P("fsdp", None, "rep", None),
            P("fsdp", None, "rep", None),
            P("fsdp", None, "rep"),
        ),
        check_vma=False,
    )
```

```python
import jax
import jax.numpy as jnp
from jax import lax
from jax.experimental import pallas as pl
from jax.experimental.pallas import tpu as pltpu
from jax.sharding import PartitionSpec as P

STAT_DECAY = 0.9


def over_core(value):
    size = lax.axis_size("rep")
    both = lax.all_gather(
        value, "rep", axis_index_groups=[[r, r + 1] for r in range(0, size, 2)]
    )
    return taken(both, 1 - lax.axis_index("rep") % 2)


def exchanged(value, mask):
    size = lax.axis_size("rep")
    return lax.ppermute(value, "rep", [(r, r ^ mask) for r in range(size)])


def passed(value, step):
    size = lax.axis_size("rep")
    return lax.ppermute(value, "rep", [(r, (r + step) % size) for r in range(size)])


def taken(value, index):
    return lax.dynamic_index_in_dim(value, index, 0, keepdims=False)


def either(first, own, other):
    return jnp.where(first, own, other), jnp.where(first, other, own)


def finish_kernel(core_ref, near_ref, far_ref, right_ref, left_ref, own_ref, given_ref, middle_ref):
    f32 = jnp.float32

    @pl.when(pl.program_id(0) == 0)
    def _():
        last = jnp.dot(far_ref[...], right_ref[...], preferred_element_type=f32)
        middle_ref[...] = (near_ref[...] + last).astype(middle_ref.dtype)

    result = jnp.dot(left_ref[0, 0], middle_ref[...], preferred_element_type=f32)
    sources, half, wide = own_ref.shape
    slab = wide // 2
    low = lax.broadcasted_iota(jnp.int32, (half, wide), 1) < slab
    for i in range(sources):
        upper = result[2 * i * half : (2 * i + 1) * half]
        lower = result[(2 * i + 1) * half : (2 * i + 2) * half]
        zero = jnp.where(low, upper, pltpu.roll(lower, slab, 1)).astype(own_ref.dtype)
        one = jnp.where(low, pltpu.roll(upper, slab, 1), lower).astype(own_ref.dtype)

        @pl.when(core_ref[0] == 0)
        def _():
            own_ref[i] = zero
            given_ref[i] = one

        @pl.when(core_ref[0] != 0)
        def _():
            own_ref[i] = one
            given_ref[i] = zero


def finish(core, near, far, right, left, sources):
    block, wide = far.shape
    half = block // sources // 2
    steps = 4
    part = jax.ShapeDtypeStruct((sources, half, wide), far.dtype)
    whole = lambda *shape: pl.BlockSpec(shape, lambda i, c: (0,) * len(shape))
    out = pl.BlockSpec((sources // steps, half, wide), lambda i, c: (i, 0, 0))
    return pl.pallas_call(
        finish_kernel,
        grid_spec=pltpu.PrefetchScalarGridSpec(
            num_scalar_prefetch=1,
            grid=(steps,),
            in_specs=[
                whole(block, wide),
                whole(block, wide),
                whole(wide, wide),
                pl.BlockSpec((1, 1, block // steps, block), lambda i, c: (0, c[0], i, 0)),
            ],
            out_specs=[out, out],
            scratch_shapes=[pltpu.VMEM((block, wide), far.dtype)],
        ),
        out_shape=[part, part],
        compiler_params=pltpu.CompilerParams(vmem_limit_bytes=24 * 2**20),
    )(core.reshape(1), near, far, right, left)


def local(grad_parts, slot_block, stat_left, stat_right, root_left, root_right):
    bf16, f32 = jnp.bfloat16, jnp.float32
    shard_rows, col_blocks = grad_parts.shape[1:3]
    block = stat_left.shape[3]
    owners, slot_count = slot_block.shape
    slab = root_right.shape[3]
    wide = 2 * slab
    chips = block // wide
    sources = block // shard_rows
    bands = owners // sources
    half = shard_rows // 2
    shard = lax.axis_index("fsdp")
    member = lax.axis_index("rep")
    core, chip = member % 2, member // 2
    first = core == 0
    my_band = shard // sources

    block_column = slot_block - my_band * col_blocks
    in_band = (slot_block >= 0) & (block_column >= 0) & (block_column < col_blocks)
    sends = jnp.any(
        in_band[:, :, None] & (block_column[:, :, None] == jnp.arange(col_blocks)), axis=1
    )
    owner_of = jnp.argmax(sends, axis=0)
    held = taken(slot_block, shard)
    held_band = held // col_blocks
    spare_band = (jnp.max(held_band) + 1) % bands
    places = jnp.where(held >= 0, held_band, spare_band).astype(jnp.uint32)
    own_place, other_place = either(first, places[0], places[1])

    partial = grad_parts[0]
    kept = lax.dynamic_slice_in_dim(partial, core * half, half, 0)
    given = lax.dynamic_slice_in_dim(partial, (1 - core) * half, half, 0)
    pair = kept.astype(f32) + over_core(given).astype(f32)
    side = chip % 2
    kept = lax.dynamic_slice_in_dim(pair, side * wide, wide, 2)
    given = lax.dynamic_slice_in_dim(pair, (1 - side) * wide, wide, 2)
    gradient = (kept + exchanged(given.astype(bf16), 2).astype(f32)).astype(bf16)

    outgoing = jnp.einsum(
        "oc,rcj->orj", sends.astype(bf16), gradient, preferred_element_type=f32
    ).astype(bf16)
    arrived = lax.all_to_all(outgoing, "fsdp", split_axis=0, concat_axis=0, tiled=True)
    blank = jnp.full((owners, half, wide), own_place // jnp.uint32(bands), bf16)
    arrived, own_place, other_place = lax.optimization_barrier(
        (arrived, own_place, other_place)
    )
    banded = arrived.reshape(bands, sources, half, wide)
    own, other = taken(banded, own_place), taken(banded, other_place)

    upper, lower = either(first, own, over_core(other))
    piece = jnp.stack([upper, lower], axis=1).reshape(block, wide)
    right_pair = either(
        first, taken(root_right[0], core), over_core(taken(root_right[0], 1 - core))
    )
    right = jnp.concatenate(right_pair, axis=1)
    right = lax.dynamic_slice_in_dim(
        jnp.concatenate([right, right], axis=0), chip * wide, block, 0
    )

    right, blank = lax.optimization_barrier((right, blank))

    up, down = [piece], [piece]
    for _ in range(chips // 2 - 1):
        up.append(passed(up[-1], 2))
        down.append(passed(down[-1], -2))
    far = jnp.concatenate(
        [passed(up[-1][: block // 2], 2), passed(down[-1][block // 2 :], -2)], axis=0
    )
    slabs = down + [far] + up[:0:-1]
    parts = [
        jnp.dot(slabs[d], right[d * wide : (d + 1) * wide], preferred_element_type=f32)
        for d in range(chips)
        if d != chips // 2
    ]
    near = parts[0] + (parts[1] + parts[6]) + (parts[2] + parts[5]) + (parts[3] + parts[4])
    own, given = finish(core, near, far, right[4 * wide : 5 * wide], root_left, sources)
    returning = blank.reshape(bands, sources, half, wide)
    returning = lax.dynamic_update_index_in_dim(returning, own, own_place, 0)
    returning = lax.dynamic_update_index_in_dim(returning, over_core(given), other_place, 0)
    returning = returning.reshape(owners, half, wide)
    *slabs, returning = lax.optimization_barrier((*slabs, returning))
    came_back = lax.all_to_all(returning, "fsdp", split_axis=0, concat_axis=0, tiled=True)
    picked = jnp.take(came_back, owner_of, axis=0)
    precond = jnp.concatenate([picked[:, :, :slab], picked[:, :, slab:]], axis=1)
    precond = precond.transpose(1, 0, 2)

    piece = slabs[0]
    whole = jnp.concatenate(slabs, axis=1)
    rows = lax.dynamic_slice_in_dim(whole, chip * wide, wide, 0)
    left_rows = jnp.einsum("ic,kc->ik", rows, whole, preferred_element_type=f32)
    right_rows = jnp.einsum("ki,kc->ic", piece, whole, preferred_element_type=f32)
    right_rows = lax.dynamic_slice_in_dim(
        jnp.concatenate([right_rows, right_rows], axis=1),
        (chips - chip) % chips * wide,
        block,
        1,
    )
    both = jnp.stack([left_rows, right_rows])
    own = lax.dynamic_slice_in_dim(both, core * slab, slab, 1)
    other = exchanged(lax.dynamic_slice_in_dim(both, (1 - core) * slab, slab, 1), 1)
    products = jnp.stack(either(first, own, other), axis=1)
    new_left = STAT_DECAY * stat_left[0] + (1.0 - STAT_DECAY) * products[0]
    new_right = STAT_DECAY * stat_right[0] + (1.0 - STAT_DECAY) * products[1]
    return (new_left[None], new_right[None], precond)


def solution(mesh):
    placed = (
        P("rep", "fsdp", None, None),
        P(),
        P("fsdp", None, "rep", None),
        P("fsdp", None, "rep", None),
        P("fsdp", None, None, None),
        P("fsdp", None, None, "rep"),
    )
    return jax.shard_map(
        local,
        mesh=mesh,
        in_specs=placed,
        out_specs=(
            P("fsdp", None, "rep", None),
            P("fsdp", None, "rep", None),
            P("fsdp", None, "rep"),
        ),
        check_vma=False,
    )
```

```python
import jax
import jax.numpy as jnp
from jax import lax
from jax.experimental import pallas as pl
from jax.experimental.pallas import tpu as pltpu
from jax.sharding import PartitionSpec as P

STAT_DECAY = 0.9


def over_core(value):
    size = lax.axis_size("rep")
    both = lax.all_gather(
        value, "rep", axis_index_groups=[[r, r + 1] for r in range(0, size, 2)]
    )
    return taken(both, 1 - lax.axis_index("rep") % 2)


def exchanged(value, mask):
    size = lax.axis_size("rep")
    return lax.ppermute(value, "rep", [(r, r ^ mask) for r in range(size)])


def passed(value, step):
    size = lax.axis_size("rep")
    return lax.ppermute(value, "rep", [(r, (r + step) % size) for r in range(size)])


def taken(value, index):
    return lax.dynamic_index_in_dim(value, index, 0, keepdims=False)


def either(first, own, other):
    return jnp.where(first, own, other), jnp.where(first, other, own)


def finish_kernel(
    core_ref, far_place_ref, own_place_ref,
    near_ref, far_ref, right_ref, left_ref, blank_ref,
    own_ref, given_ref, middle_ref,
):
    f32 = jnp.float32

    @pl.when(pl.program_id(0) == 0)
    def _():
        last = jnp.dot(far_ref[...], right_ref[0], preferred_element_type=f32)
        middle_ref[...] = (near_ref[...] + last).astype(middle_ref.dtype)

    result = jnp.dot(left_ref[0, 0], middle_ref[...], preferred_element_type=f32)
    sources, half, wide = given_ref.shape
    slab = wide // 2
    low = lax.broadcasted_iota(jnp.int32, (half, wide), 1) < slab
    for i in range(sources):
        upper = result[2 * i * half : (2 * i + 1) * half]
        lower = result[(2 * i + 1) * half : (2 * i + 2) * half]
        zero = jnp.where(low, upper, pltpu.roll(lower, slab, 1)).astype(given_ref.dtype)
        one = jnp.where(low, pltpu.roll(upper, slab, 1), lower).astype(given_ref.dtype)

        @pl.when(core_ref[0] == 0)
        def _():
            own_ref[0, i] = zero
            given_ref[i] = one

        @pl.when(core_ref[0] != 0)
        def _():
            own_ref[0, i] = one
            given_ref[i] = zero


def finish(core, far_place, own_place, near, far, right, left, blank):
    block, wide = far.shape
    _, sources, half, _ = blank.shape
    steps = 4
    few = sources // steps
    return pl.pallas_call(
        finish_kernel,
        grid_spec=pltpu.PrefetchScalarGridSpec(
            num_scalar_prefetch=3,
            grid=(steps,),
            in_specs=[
                pl.BlockSpec((block, wide), lambda i, c, f, o: (0, 0)),
                pl.BlockSpec((block, wide), lambda i, c, f, o: (0, 0)),
                pl.BlockSpec((1, wide, wide), lambda i, c, f, o: (f[0], 0, 0)),
                pl.BlockSpec((1, 1, block // steps, block), lambda i, c, f, o: (0, c[0], i, 0)),
                pl.BlockSpec(memory_space=pl.ANY),
            ],
            out_specs=[
                pl.BlockSpec((1, few, half, wide), lambda i, c, f, o: (o[0], i, 0, 0)),
                pl.BlockSpec((few, half, wide), lambda i, c, f, o: (i, 0, 0)),
            ],
            scratch_shapes=[pltpu.VMEM((block, wide), far.dtype)],
        ),
        out_shape=[
            jax.ShapeDtypeStruct(blank.shape, blank.dtype),
            jax.ShapeDtypeStruct((sources, half, wide), far.dtype),
        ],
        input_output_aliases={7: 0},
        compiler_params=pltpu.CompilerParams(vmem_limit_bytes=24 * 2**20),
    )(core.reshape(1), far_place.reshape(1), own_place.reshape(1), near, far, right, left, blank)


def local(grad_parts, slot_block, stat_left, stat_right, root_left, root_right):
    bf16, f32 = jnp.bfloat16, jnp.float32
    shard_rows, col_blocks = grad_parts.shape[1:3]
    block = stat_left.shape[3]
    owners, slot_count = slot_block.shape
    slab = root_right.shape[3]
    wide = 2 * slab
    chips = block // wide
    sources = block // shard_rows
    bands = owners // sources
    half = shard_rows // 2
    shard = lax.axis_index("fsdp")
    member = lax.axis_index("rep")
    core, chip = member % 2, member // 2
    first = core == 0
    my_band = shard // sources

    block_column = slot_block - my_band * col_blocks
    in_band = (slot_block >= 0) & (block_column >= 0) & (block_column < col_blocks)
    sends = jnp.any(
        in_band[:, :, None] & (block_column[:, :, None] == jnp.arange(col_blocks)), axis=1
    )
    owner_of = jnp.argmax(sends, axis=0)
    held = taken(slot_block, shard)
    held_band = held // col_blocks
    spare_band = (jnp.max(held_band) + 1) % bands
    places = jnp.where(held >= 0, held_band, spare_band).astype(jnp.uint32)
    own_place, other_place = either(first, places[0], places[1])

    partial = grad_parts[0]
    kept = lax.dynamic_slice_in_dim(partial, core * half, half, 0)
    given = lax.dynamic_slice_in_dim(partial, (1 - core) * half, half, 0)
    pair = kept.astype(f32) + over_core(given).astype(f32)
    side = chip % 2
    kept = lax.dynamic_slice_in_dim(pair, side * wide, wide, 2)
    given = lax.dynamic_slice_in_dim(pair, (1 - side) * wide, wide, 2)
    gradient = (kept + exchanged(given.astype(bf16), 2).astype(f32)).astype(bf16)

    outgoing = jnp.einsum(
        "oc,rcj->orj", sends.astype(bf16), gradient, preferred_element_type=f32
    ).astype(bf16)
    arrived = lax.all_to_all(outgoing, "fsdp", split_axis=0, concat_axis=0, tiled=True)
    blank = jnp.full((owners, half, wide), own_place // jnp.uint32(bands), bf16)
    arrived, own_place, other_place = lax.optimization_barrier(
        (arrived, own_place, other_place)
    )
    banded = arrived.reshape(bands, sources, half, wide)
    own, other = taken(banded, own_place), taken(banded, other_place)

    upper, lower = either(first, own, over_core(other))
    piece = jnp.stack([upper, lower], axis=1).reshape(block, wide)
    right_pair = either(
        first, taken(root_right[0], core), over_core(taken(root_right[0], 1 - core))
    )
    right = jnp.concatenate(right_pair, axis=1).reshape(chips, wide, wide)

    up, down = [piece], [piece]
    for _ in range(chips // 2 - 1):
        up.append(passed(up[-1], 2))
        down.append(passed(down[-1], -2))
    far = jnp.concatenate(
        [passed(up[-1][: block // 2], 2), passed(down[-1][block // 2 :], -2)], axis=0
    )
    def part(away, columns):
        rows = taken(right, ((chip + away) % chips).astype(jnp.uint32))
        return jnp.dot(columns, rows, preferred_element_type=f32)

    near = part(0, piece)
    for away in range(1, chips // 2):
        near = near + (part(away, down[away]) + part(chips - away, up[away]))
        if away == 1:
            near, blank = lax.optimization_barrier((near, blank))

    blank = blank.reshape(bands, sources, half, wide)
    far_place = (chip + chips // 2) % chips
    returning, given = finish(
        core, far_place, own_place.astype(jnp.int32), near, far, right, root_left, blank
    )
    returning = lax.dynamic_update_index_in_dim(returning, over_core(given), other_place, 0)
    returning = returning.reshape(owners, half, wide)
    slabs = down + [far] + up[:0:-1]
    *slabs, returning = lax.optimization_barrier((*slabs, returning))
    came_back = lax.all_to_all(returning, "fsdp", split_axis=0, concat_axis=0, tiled=True)
    picked = jnp.take(came_back, owner_of, axis=0)
    precond = jnp.concatenate([picked[:, :, :slab], picked[:, :, slab:]], axis=1)
    precond = precond.transpose(1, 0, 2)

    piece = slabs[0]
    whole = jnp.concatenate(slabs, axis=1)
    rows = lax.dynamic_slice_in_dim(whole, chip * wide, wide, 0)
    left_rows = jnp.einsum("ic,kc->ik", rows, whole, preferred_element_type=f32)
    right_rows = jnp.einsum("ki,kc->ic", piece, whole, preferred_element_type=f32)
    right_rows = lax.dynamic_slice_in_dim(
        jnp.concatenate([right_rows, right_rows], axis=1),
        (chips - chip) % chips * wide,
        block,
        1,
    )
    both = jnp.stack([left_rows, right_rows])
    own = lax.dynamic_slice_in_dim(both, core * slab, slab, 1)
    other = exchanged(lax.dynamic_slice_in_dim(both, (1 - core) * slab, slab, 1), 1)
    products = jnp.stack(either(first, own, other), axis=1)
    new_left = STAT_DECAY * stat_left[0] + (1.0 - STAT_DECAY) * products[0]
    new_right = STAT_DECAY * stat_right[0] + (1.0 - STAT_DECAY) * products[1]
    return (new_left[None], new_right[None], precond)


def solution(mesh):
    placed = (
        P("rep", "fsdp", None, None),
        P(),
        P("fsdp", None, "rep", None),
        P("fsdp", None, "rep", None),
        P("fsdp", None, None, None),
        P("fsdp", None, None, "rep"),
    )
    return jax.shard_map(
        local,
        mesh=mesh,
        in_specs=placed,
        out_specs=(
            P("fsdp", None, "rep", None),
            P("fsdp", None, "rep", None),
            P("fsdp", None, "rep"),
        ),
        check_vma=False,
    )
```

```python
import jax
import jax.numpy as jnp
from jax import lax
from jax.experimental import pallas as pl
from jax.experimental.pallas import tpu as pltpu
from jax.sharding import PartitionSpec as P

STAT_DECAY = 0.9


def over_core(value):
    size = lax.axis_size("rep")
    both = lax.all_gather(
        value, "rep", axis_index_groups=[[r, r + 1] for r in range(0, size, 2)]
    )
    return taken(both, 1 - lax.axis_index("rep") % 2)


def exchanged(value, mask):
    size = lax.axis_size("rep")
    return lax.ppermute(value, "rep", [(r, r ^ mask) for r in range(size)])


def passed(value, step):
    size = lax.axis_size("rep")
    return lax.ppermute(value, "rep", [(r, (r + step) % size) for r in range(size)])


def taken(value, index):
    return lax.dynamic_index_in_dim(value, index, 0, keepdims=False)


def either(first, own, other):
    return jnp.where(first, own, other), jnp.where(first, other, own)


def finish_kernel(
    core_ref, far_place_ref, own_place_ref,
    near_ref, far_ref, right_ref, left_ref, blank_ref,
    own_ref, given_ref, middle_ref,
):
    f32 = jnp.float32

    @pl.when(pl.program_id(0) == 0)
    def _():
        last = jnp.dot(far_ref[...], right_ref[0], preferred_element_type=f32)
        middle_ref[...] = (near_ref[...] + last).astype(middle_ref.dtype)

    result = jnp.dot(left_ref[0, 0], middle_ref[...], preferred_element_type=f32)
    sources, half, wide = given_ref.shape
    slab = wide // 2
    low = lax.broadcasted_iota(jnp.int32, (half, wide), 1) < slab
    for i in range(sources):
        upper = result[2 * i * half : (2 * i + 1) * half]
        lower = result[(2 * i + 1) * half : (2 * i + 2) * half]
        zero = jnp.where(low, upper, pltpu.roll(lower, slab, 1)).astype(given_ref.dtype)
        one = jnp.where(low, pltpu.roll(upper, slab, 1), lower).astype(given_ref.dtype)

        @pl.when(core_ref[0] == 0)
        def _():
            own_ref[0, i] = zero
            given_ref[i] = one

        @pl.when(core_ref[0] != 0)
        def _():
            own_ref[0, i] = one
            given_ref[i] = zero


def finish(core, far_place, own_place, near, far, right, left, blank):
    block, wide = far.shape
    _, sources, half, _ = blank.shape
    steps = 4
    few = sources // steps
    return pl.pallas_call(
        finish_kernel,
        grid_spec=pltpu.PrefetchScalarGridSpec(
            num_scalar_prefetch=3,
            grid=(steps,),
            in_specs=[
                pl.BlockSpec((block, wide), lambda i, c, f, o: (0, 0)),
                pl.BlockSpec((block, wide), lambda i, c, f, o: (0, 0)),
                pl.BlockSpec((1, wide, wide), lambda i, c, f, o: (f[0], 0, 0)),
                pl.BlockSpec((1, 1, block // steps, block), lambda i, c, f, o: (0, c[0], i, 0)),
                pl.BlockSpec(memory_space=pl.ANY),
            ],
            out_specs=[
                pl.BlockSpec((1, few, half, wide), lambda i, c, f, o: (o[0], i, 0, 0)),
                pl.BlockSpec((few, half, wide), lambda i, c, f, o: (i, 0, 0)),
            ],
            scratch_shapes=[pltpu.VMEM((block, wide), far.dtype)],
        ),
        out_shape=[
            jax.ShapeDtypeStruct(blank.shape, blank.dtype),
            jax.ShapeDtypeStruct((sources, half, wide), far.dtype),
        ],
        input_output_aliases={7: 0},
        compiler_params=pltpu.CompilerParams(vmem_limit_bytes=24 * 2**20),
    )(core.reshape(1), far_place.reshape(1), own_place.reshape(1), near, far, right, left, blank)


def local(grad_parts, slot_block, stat_left, stat_right, root_left, root_right):
    bf16, f32 = jnp.bfloat16, jnp.float32
    shard_rows, col_blocks = grad_parts.shape[1:3]
    block = stat_left.shape[3]
    owners, slot_count = slot_block.shape
    slab = root_right.shape[3]
    wide = 2 * slab
    chips = block // wide
    sources = block // shard_rows
    bands = owners // sources
    half = shard_rows // 2
    shard = lax.axis_index("fsdp")
    member = lax.axis_index("rep")
    core, chip = member % 2, member // 2
    first = core == 0
    my_band = shard // sources

    block_column = slot_block - my_band * col_blocks
    in_band = (slot_block >= 0) & (block_column >= 0) & (block_column < col_blocks)
    sends = jnp.any(
        in_band[:, :, None] & (block_column[:, :, None] == jnp.arange(col_blocks)), axis=1
    )
    owner_of = jnp.argmax(sends, axis=0)
    held = taken(slot_block, shard)
    held_band = held // col_blocks
    spare_band = (jnp.max(held_band) + 1) % bands
    places = jnp.where(held >= 0, held_band, spare_band).astype(jnp.uint32)
    own_place, other_place = either(first, places[0], places[1])

    partial = grad_parts[0]
    kept = lax.dynamic_slice_in_dim(partial, core * half, half, 0)
    given = lax.dynamic_slice_in_dim(partial, (1 - core) * half, half, 0)
    pair = kept.astype(f32) + over_core(given).astype(f32)
    side = chip % 2
    kept = lax.dynamic_slice_in_dim(pair, side * wide, wide, 2)
    given = lax.dynamic_slice_in_dim(pair, (1 - side) * wide, wide, 2)
    gradient = (kept + exchanged(given.astype(bf16), 2).astype(f32)).astype(bf16)

    outgoing = jnp.einsum(
        "oc,rcj->orj", sends.astype(bf16), gradient, preferred_element_type=f32
    ).astype(bf16)
    arrived = lax.all_to_all(outgoing, "fsdp", split_axis=0, concat_axis=0, tiled=True)
    blank = jnp.full((owners, half, wide), own_place // jnp.uint32(bands), bf16)
    arrived, own_place, other_place = lax.optimization_barrier(
        (arrived, own_place, other_place)
    )
    banded = arrived.reshape(bands, sources, half, wide)
    own, other = taken(banded, own_place), taken(banded, other_place)

    upper, lower = either(first, own, over_core(other))
    piece = jnp.stack([upper, lower], axis=1).reshape(block, wide)
    right_pair = either(
        first, taken(root_right[0], core), over_core(taken(root_right[0], 1 - core))
    )
    right = jnp.concatenate(right_pair, axis=1).reshape(chips, wide, wide)

    up, down = [piece], [piece]
    for _ in range(chips // 2 - 1):
        up.append(passed(up[-1], 2))
        down.append(passed(down[-1], -2))
    far = passed(up[-1], 2)

    def part(away, columns):
        rows = taken(right, ((chip + away) % chips).astype(jnp.uint32))
        return jnp.dot(columns, rows, preferred_element_type=f32)

    near = part(0, piece)
    for away in range(1, chips // 2):
        near = near + (part(away, down[away]) + part(chips - away, up[away]))
        if away == 1:
            near, blank = lax.optimization_barrier((near, blank))

    blank = blank.reshape(bands, sources, half, wide)
    far_place = (chip + chips // 2) % chips
    returning, given = finish(
        core, far_place, own_place.astype(jnp.int32), near, far, right, root_left, blank
    )
    returning = lax.dynamic_update_index_in_dim(returning, over_core(given), other_place, 0)
    returning = returning.reshape(owners, half, wide)
    slabs = down + [far] + up[:0:-1]
    *slabs, returning = lax.optimization_barrier((*slabs, returning))
    came_back = lax.all_to_all(returning, "fsdp", split_axis=0, concat_axis=0, tiled=True)
    picked = jnp.take(came_back, owner_of, axis=0)
    precond = jnp.concatenate([picked[:, :, :slab], picked[:, :, slab:]], axis=1)
    precond = precond.transpose(1, 0, 2)

    piece = slabs[0]
    whole = jnp.concatenate(slabs, axis=1)
    rows = lax.dynamic_slice_in_dim(whole, chip * wide, wide, 0)
    left_rows = jnp.einsum("ic,kc->ik", rows, whole, preferred_element_type=f32)
    right_rows = jnp.einsum("ki,kc->ic", piece, whole, preferred_element_type=f32)
    right_rows = lax.dynamic_slice_in_dim(
        jnp.concatenate([right_rows, right_rows], axis=1),
        (chips - chip) % chips * wide,
        block,
        1,
    )
    both = jnp.stack([left_rows, right_rows])
    own = lax.dynamic_slice_in_dim(both, core * slab, slab, 1)
    other = exchanged(lax.dynamic_slice_in_dim(both, (1 - core) * slab, slab, 1), 1)
    products = jnp.stack(either(first, own, other), axis=1)
    new_left = STAT_DECAY * stat_left[0] + (1.0 - STAT_DECAY) * products[0]
    new_right = STAT_DECAY * stat_right[0] + (1.0 - STAT_DECAY) * products[1]
    return (new_left[None], new_right[None], precond)


def solution(mesh):
    placed = (
        P("rep", "fsdp", None, None),
        P(),
        P("fsdp", None, "rep", None),
        P("fsdp", None, "rep", None),
        P("fsdp", None, None, None),
        P("fsdp", None, None, "rep"),
    )
    return jax.shard_map(
        local,
        mesh=mesh,
        in_specs=placed,
        out_specs=(
            P("fsdp", None, "rep", None),
            P("fsdp", None, "rep", None),
            P("fsdp", None, "rep"),
        ),
        check_vma=False,
    )
```

```python
import jax
import jax.numpy as jnp
from jax import lax
from jax.experimental import pallas as pl
from jax.experimental.pallas import tpu as pltpu
from jax.sharding import PartitionSpec as P

STAT_DECAY = 0.9


def over_core(value):
    size = lax.axis_size("rep")
    both = lax.all_gather(
        value, "rep", axis_index_groups=[[r, r + 1] for r in range(0, size, 2)]
    )
    return taken(both, 1 - lax.axis_index("rep") % 2)


def exchanged(value, mask):
    size = lax.axis_size("rep")
    return lax.ppermute(value, "rep", [(r, r ^ mask) for r in range(size)])


def passed(value, step):
    size = lax.axis_size("rep")
    return lax.ppermute(value, "rep", [(r, (r + step) % size) for r in range(size)])


def taken(value, index):
    return lax.dynamic_index_in_dim(value, index, 0, keepdims=False)


def either(first, own, other):
    return jnp.where(first, own, other), jnp.where(first, other, own)


def finish_kernel(
    core_ref, far_place_ref, own_place_ref,
    near_ref, far_ref, right_ref, left_ref, blank_ref,
    own_ref, given_ref, middle_ref,
):
    f32 = jnp.float32

    @pl.when(pl.program_id(0) == 0)
    def _():
        last = jnp.dot(far_ref[...], right_ref[0], preferred_element_type=f32)
        middle_ref[...] = (near_ref[...] + last).astype(middle_ref.dtype)

    result = jnp.dot(left_ref[0, 0], middle_ref[...], preferred_element_type=f32)
    sources, half, wide = given_ref.shape
    slab = wide // 2
    low = lax.broadcasted_iota(jnp.int32, (half, wide), 1) < slab
    for i in range(sources):
        upper = result[2 * i * half : (2 * i + 1) * half]
        lower = result[(2 * i + 1) * half : (2 * i + 2) * half]
        zero = jnp.where(low, upper, pltpu.roll(lower, slab, 1)).astype(given_ref.dtype)
        one = jnp.where(low, pltpu.roll(upper, slab, 1), lower).astype(given_ref.dtype)

        @pl.when(core_ref[0] == 0)
        def _():
            own_ref[0, i] = zero
            given_ref[i] = one

        @pl.when(core_ref[0] != 0)
        def _():
            own_ref[0, i] = one
            given_ref[i] = zero


def finish(core, far_place, own_place, near, far, right, left, blank):
    block, wide = far.shape
    _, sources, half, _ = blank.shape
    steps = 4
    few = sources // steps
    return pl.pallas_call(
        finish_kernel,
        grid_spec=pltpu.PrefetchScalarGridSpec(
            num_scalar_prefetch=3,
            grid=(steps,),
            in_specs=[
                pl.BlockSpec((block, wide), lambda i, c, f, o: (0, 0)),
                pl.BlockSpec((block, wide), lambda i, c, f, o: (0, 0)),
                pl.BlockSpec((1, wide, wide), lambda i, c, f, o: (f[0], 0, 0)),
                pl.BlockSpec((1, 1, block // steps, block), lambda i, c, f, o: (0, c[0], i, 0)),
                pl.BlockSpec(memory_space=pl.ANY),
            ],
            out_specs=[
                pl.BlockSpec((1, few, half, wide), lambda i, c, f, o: (o[0], i, 0, 0)),
                pl.BlockSpec((few, half, wide), lambda i, c, f, o: (i, 0, 0)),
            ],
            scratch_shapes=[pltpu.VMEM((block, wide), far.dtype)],
        ),
        out_shape=[
            jax.ShapeDtypeStruct(blank.shape, blank.dtype),
            jax.ShapeDtypeStruct((sources, half, wide), far.dtype),
        ],
        input_output_aliases={7: 0},
        compiler_params=pltpu.CompilerParams(vmem_limit_bytes=24 * 2**20),
    )(core.reshape(1), far_place.reshape(1), own_place.reshape(1), near, far, right, left, blank)


def local(grad_parts, slot_block, stat_left, stat_right, root_left, root_right):
    bf16, f32 = jnp.bfloat16, jnp.float32
    shard_rows, col_blocks = grad_parts.shape[1:3]
    block = stat_left.shape[3]
    owners, slot_count = slot_block.shape
    slab = root_right.shape[3]
    wide = 2 * slab
    chips = block // wide
    sources = block // shard_rows
    bands = owners // sources
    half = shard_rows // 2
    shard = lax.axis_index("fsdp")
    member = lax.axis_index("rep")
    core, chip = member % 2, member // 2
    first = core == 0
    my_band = shard // sources

    block_column = slot_block - my_band * col_blocks
    in_band = (slot_block >= 0) & (block_column >= 0) & (block_column < col_blocks)
    sends = jnp.any(
        in_band[:, :, None] & (block_column[:, :, None] == jnp.arange(col_blocks)), axis=1
    )
    owner_of = jnp.argmax(sends, axis=0)
    held = taken(slot_block, shard)
    held_band = held // col_blocks
    spare_band = (jnp.max(held_band) + 1) % bands
    places = jnp.where(held >= 0, held_band, spare_band).astype(jnp.uint32)
    own_place, other_place = either(first, places[0], places[1])

    partial = grad_parts[0]
    kept = lax.dynamic_slice_in_dim(partial, core * half, half, 0)
    given = lax.dynamic_slice_in_dim(partial, (1 - core) * half, half, 0)
    pair = kept.astype(f32) + over_core(given).astype(f32)
    side = chip % 2
    kept = lax.dynamic_slice_in_dim(pair, side * wide, wide, 2)
    given = lax.dynamic_slice_in_dim(pair, (1 - side) * wide, wide, 2)
    gradient = (kept + exchanged(given.astype(bf16), 2).astype(f32)).astype(bf16)

    outgoing = jnp.einsum(
        "oc,rcj->orj", sends.astype(bf16), gradient, preferred_element_type=f32
    ).astype(bf16)
    arrived = lax.all_to_all(outgoing, "fsdp", split_axis=0, concat_axis=0, tiled=True)
    blank = jnp.full((owners, half, wide), own_place // jnp.uint32(bands), bf16)
    arrived, own_place, other_place = lax.optimization_barrier(
        (arrived, own_place, other_place)
    )
    banded = arrived.reshape(bands, sources, half, wide)
    own, other = taken(banded, own_place), taken(banded, other_place)

    upper, lower = either(first, own, over_core(other))
    piece = jnp.stack([upper, lower], axis=1).reshape(block, wide)
    right_pair = either(
        first, taken(root_right[0], core), over_core(taken(root_right[0], 1 - core))
    )
    right = jnp.concatenate(right_pair, axis=1).reshape(chips, wide, wide)

    up, down = [piece], [piece]
    for _ in range(chips // 2 - 1):
        up.append(passed(up[-1], 2))
        down.append(passed(down[-1], -2))
    size = lax.axis_size("rep")
    pairs = [(r, (r + (2 if r % 2 == 0 else -2)) % size) for r in range(size)]
    far = lax.ppermute(jnp.where(first, up[-1], down[-1]), "rep", pairs)

    def part(away, columns):
        rows = taken(right, ((chip + away) % chips).astype(jnp.uint32))
        return jnp.dot(columns, rows, preferred_element_type=f32)

    near = part(0, piece)
    for away in range(1, chips // 2):
        near = near + (part(away, down[away]) + part(chips - away, up[away]))
        if away == 1:
            near, blank = lax.optimization_barrier((near, blank))

    blank = blank.reshape(bands, sources, half, wide)
    far_place = (chip + chips // 2) % chips
    returning, given = finish(
        core, far_place, own_place.astype(jnp.int32), near, far, right, root_left, blank
    )
    returning = lax.dynamic_update_index_in_dim(returning, over_core(given), other_place, 0)
    returning = returning.reshape(owners, half, wide)
    slabs = down + [far] + up[:0:-1]
    *slabs, returning = lax.optimization_barrier((*slabs, returning))
    came_back = lax.all_to_all(returning, "fsdp", split_axis=0, concat_axis=0, tiled=True)
    picked = jnp.take(came_back, owner_of, axis=0)
    precond = jnp.concatenate([picked[:, :, :slab], picked[:, :, slab:]], axis=1)
    precond = precond.transpose(1, 0, 2)

    piece = slabs[0]
    whole = jnp.concatenate(slabs, axis=1)
    rows = lax.dynamic_slice_in_dim(whole, chip * wide, wide, 0)
    left_rows = jnp.einsum("ic,kc->ik", rows, whole, preferred_element_type=f32)
    right_rows = jnp.einsum("ki,kc->ic", piece, whole, preferred_element_type=f32)
    right_rows = lax.dynamic_slice_in_dim(
        jnp.concatenate([right_rows, right_rows], axis=1),
        (chips - chip) % chips * wide,
        block,
        1,
    )
    both = jnp.stack([left_rows, right_rows])
    own = lax.dynamic_slice_in_dim(both, core * slab, slab, 1)
    other = exchanged(lax.dynamic_slice_in_dim(both, (1 - core) * slab, slab, 1), 1)
    products = jnp.stack(either(first, own, other), axis=1)
    new_left = STAT_DECAY * stat_left[0] + (1.0 - STAT_DECAY) * products[0]
    new_right = STAT_DECAY * stat_right[0] + (1.0 - STAT_DECAY) * products[1]
    return (new_left[None], new_right[None], precond)


def solution(mesh):
    placed = (
        P("rep", "fsdp", None, None),
        P(),
        P("fsdp", None, "rep", None),
        P("fsdp", None, "rep", None),
        P("fsdp", None, None, None),
        P("fsdp", None, None, "rep"),
    )
    return jax.shard_map(
        local,
        mesh=mesh,
        in_specs=placed,
        out_specs=(
            P("fsdp", None, "rep", None),
            P("fsdp", None, "rep", None),
            P("fsdp", None, "rep"),
        ),
        check_vma=False,
    )
```

```python
import jax
import jax.numpy as jnp
from jax import lax
from jax.experimental import pallas as pl
from jax.experimental.pallas import tpu as pltpu
from jax.sharding import PartitionSpec as P

STAT_DECAY = 0.9


def over_core(value):
    size = lax.axis_size("rep")
    both = lax.all_gather(
        value, "rep", axis_index_groups=[[r, r + 1] for r in range(0, size, 2)]
    )
    return taken(both, 1 - lax.axis_index("rep") % 2)


def exchanged(value, mask):
    size = lax.axis_size("rep")
    return lax.ppermute(value, "rep", [(r, r ^ mask) for r in range(size)])


def passed(value, step):
    size = lax.axis_size("rep")
    return lax.ppermute(value, "rep", [(r, (r + step) % size) for r in range(size)])


def taken(value, index):
    return lax.dynamic_index_in_dim(value, index, 0, keepdims=False)


def either(first, own, other):
    return jnp.where(first, own, other), jnp.where(first, other, own)


def finish_kernel(
    core_ref, far_place_ref, own_place_ref,
    near_ref, far_ref, right_ref, left_ref, blank_ref,
    own_ref, given_ref, middle_ref,
):
    f32 = jnp.float32

    @pl.when(pl.program_id(0) == 0)
    def _():
        last = jnp.dot(far_ref[...], right_ref[0], preferred_element_type=f32)
        middle_ref[...] = (near_ref[...] + last).astype(middle_ref.dtype)

    result = jnp.dot(left_ref[0, 0], middle_ref[...], preferred_element_type=f32)
    sources, half, wide = given_ref.shape
    slab = wide // 2
    low = lax.broadcasted_iota(jnp.int32, (half, wide), 1) < slab
    for i in range(sources):
        upper = result[2 * i * half : (2 * i + 1) * half]
        lower = result[(2 * i + 1) * half : (2 * i + 2) * half]
        zero = jnp.where(low, upper, pltpu.roll(lower, slab, 1)).astype(given_ref.dtype)
        one = jnp.where(low, pltpu.roll(upper, slab, 1), lower).astype(given_ref.dtype)

        @pl.when(core_ref[0] == 0)
        def _():
            own_ref[0, i] = zero
            given_ref[i] = one

        @pl.when(core_ref[0] != 0)
        def _():
            own_ref[0, i] = one
            given_ref[i] = zero


def finish(core, far_place, own_place, near, far, right, left, blank):
    block, wide = far.shape
    _, sources, half, _ = blank.shape
    steps = 4
    few = sources // steps
    return pl.pallas_call(
        finish_kernel,
        grid_spec=pltpu.PrefetchScalarGridSpec(
            num_scalar_prefetch=3,
            grid=(steps,),
            in_specs=[
                pl.BlockSpec((block, wide), lambda i, c, f, o: (0, 0)),
                pl.BlockSpec((block, wide), lambda i, c, f, o: (0, 0)),
                pl.BlockSpec((1, wide, wide), lambda i, c, f, o: (f[0], 0, 0)),
                pl.BlockSpec((1, 1, block // steps, block), lambda i, c, f, o: (0, c[0], i, 0)),
                pl.BlockSpec(memory_space=pl.ANY),
            ],
            out_specs=[
                pl.BlockSpec((1, few, half, wide), lambda i, c, f, o: (o[0], i, 0, 0)),
                pl.BlockSpec((few, half, wide), lambda i, c, f, o: (i, 0, 0)),
            ],
            scratch_shapes=[pltpu.VMEM((block, wide), far.dtype)],
        ),
        out_shape=[
            jax.ShapeDtypeStruct(blank.shape, blank.dtype),
            jax.ShapeDtypeStruct((sources, half, wide), far.dtype),
        ],
        input_output_aliases={7: 0},
        compiler_params=pltpu.CompilerParams(vmem_limit_bytes=24 * 2**20),
    )(core.reshape(1), far_place.reshape(1), own_place.reshape(1), near, far, right, left, blank)


def place_kernel(owner_ref, back_ref, out_ref):
    half = back_ref.shape[1]
    col_blocks, slab = out_ref.shape[1:]
    picked = jnp.stack(
        [back_ref[owner_ref[c]].astype(jnp.float32) for c in range(col_blocks)]
    )
    picked = jnp.swapaxes(picked, 0, 1)
    out_ref[:half] = picked[:, :, :slab].astype(out_ref.dtype)
    out_ref[half:] = picked[:, :, slab:].astype(out_ref.dtype)


def place(owner_of, came_back, col_blocks):
    _, half, wide = came_back.shape
    shape = (2 * half, col_blocks, wide // 2)
    return pl.pallas_call(
        place_kernel,
        grid_spec=pltpu.PrefetchScalarGridSpec(
            num_scalar_prefetch=1,
            grid=(1,),
            in_specs=[pl.BlockSpec(came_back.shape, lambda i, o: (0, 0, 0))],
            out_specs=pl.BlockSpec(shape, lambda i, o: (0, 0, 0)),
        ),
        out_shape=jax.ShapeDtypeStruct(shape, came_back.dtype),
        compiler_params=pltpu.CompilerParams(vmem_limit_bytes=16 * 2**20),
    )(owner_of.astype(jnp.int32), came_back)


def local(grad_parts, slot_block, stat_left, stat_right, root_left, root_right):
    bf16, f32 = jnp.bfloat16, jnp.float32
    shard_rows, col_blocks = grad_parts.shape[1:3]
    block = stat_left.shape[3]
    owners, slot_count = slot_block.shape
    slab = root_right.shape[3]
    wide = 2 * slab
    chips = block // wide
    sources = block // shard_rows
    bands = owners // sources
    half = shard_rows // 2
    shard = lax.axis_index("fsdp")
    member = lax.axis_index("rep")
    core, chip = member % 2, member // 2
    first = core == 0
    my_band = shard // sources

    block_column = slot_block - my_band * col_blocks
    in_band = (slot_block >= 0) & (block_column >= 0) & (block_column < col_blocks)
    sends = jnp.any(
        in_band[:, :, None] & (block_column[:, :, None] == jnp.arange(col_blocks)), axis=1
    )
    owner_of = jnp.argmax(sends, axis=0)
    held = taken(slot_block, shard)
    held_band = held // col_blocks
    spare_band = (jnp.max(held_band) + 1) % bands
    places = jnp.where(held >= 0, held_band, spare_band).astype(jnp.uint32)
    own_place, other_place = either(first, places[0], places[1])

    partial = grad_parts[0]
    kept = lax.dynamic_slice_in_dim(partial, core * half, half, 0)
    given = lax.dynamic_slice_in_dim(partial, (1 - core) * half, half, 0)
    pair = kept.astype(f32) + over_core(given).astype(f32)
    side = chip % 2
    kept = lax.dynamic_slice_in_dim(pair, side * wide, wide, 2)
    given = lax.dynamic_slice_in_dim(pair, (1 - side) * wide, wide, 2)
    gradient = (kept + exchanged(given.astype(bf16), 2).astype(f32)).astype(bf16)

    outgoing = jnp.einsum(
        "oc,rcj->orj", sends.astype(bf16), gradient, preferred_element_type=f32
    ).astype(bf16)
    arrived = lax.all_to_all(outgoing, "fsdp", split_axis=0, concat_axis=0, tiled=True)
    blank = jnp.full((owners, half, wide), own_place // jnp.uint32(bands), bf16)
    arrived, own_place, other_place = lax.optimization_barrier(
        (arrived, own_place, other_place)
    )
    banded = arrived.reshape(bands, sources, half, wide)
    own, other = taken(banded, own_place), taken(banded, other_place)

    upper, lower = either(first, own, over_core(other))
    piece = jnp.stack([upper, lower], axis=1).reshape(block, wide)
    right_pair = either(
        first, taken(root_right[0], core), over_core(taken(root_right[0], 1 - core))
    )
    right = jnp.concatenate(right_pair, axis=1).reshape(chips, wide, wide)

    up, down = [piece], [piece]
    for _ in range(chips // 2 - 1):
        up.append(passed(up[-1], 2))
        down.append(passed(down[-1], -2))
    far = passed(up[-1], 2)

    def part(away, columns):
        rows = taken(right, ((chip + away) % chips).astype(jnp.uint32))
        return jnp.dot(columns, rows, preferred_element_type=f32)

    near = part(0, piece)
    for away in range(1, chips // 2):
        near = near + (part(away, down[away]) + part(chips - away, up[away]))
        if away == 1:
            near, blank = lax.optimization_barrier((near, blank))

    blank = blank.reshape(bands, sources, half, wide)
    far_place = (chip + chips // 2) % chips
    returning, given = finish(
        core, far_place, own_place.astype(jnp.int32), near, far, right, root_left, blank
    )
    returning = lax.dynamic_update_index_in_dim(returning, over_core(given), other_place, 0)
    returning = returning.reshape(owners, half, wide)
    slabs = down + [far] + up[:0:-1]
    *slabs, returning = lax.optimization_barrier((*slabs, returning))
    came_back = lax.all_to_all(returning, "fsdp", split_axis=0, concat_axis=0, tiled=True)
    precond = place(owner_of, came_back, col_blocks)

    piece = slabs[0]
    whole = jnp.concatenate(slabs, axis=1)
    rows = lax.dynamic_slice_in_dim(whole, chip * wide, wide, 0)
    left_rows = jnp.einsum("ic,kc->ik", rows, whole, preferred_element_type=f32)
    right_rows = jnp.einsum("ki,kc->ic", piece, whole, preferred_element_type=f32)
    right_rows = lax.dynamic_slice_in_dim(
        jnp.concatenate([right_rows, right_rows], axis=1),
        (chips - chip) % chips * wide,
        block,
        1,
    )
    both = jnp.stack([left_rows, right_rows])
    own = lax.dynamic_slice_in_dim(both, core * slab, slab, 1)
    other = exchanged(lax.dynamic_slice_in_dim(both, (1 - core) * slab, slab, 1), 1)
    products = jnp.stack(either(first, own, other), axis=1)
    new_left = STAT_DECAY * stat_left[0] + (1.0 - STAT_DECAY) * products[0]
    new_right = STAT_DECAY * stat_right[0] + (1.0 - STAT_DECAY) * products[1]
    return (new_left[None], new_right[None], precond)


def solution(mesh):
    placed = (
        P("rep", "fsdp", None, None),
        P(),
        P("fsdp", None, "rep", None),
        P("fsdp", None, "rep", None),
        P("fsdp", None, None, None),
        P("fsdp", None, None, "rep"),
    )
    return jax.shard_map(
        local,
        mesh=mesh,
        in_specs=placed,
        out_specs=(
            P("fsdp", None, "rep", None),
            P("fsdp", None, "rep", None),
            P("fsdp", None, "rep"),
        ),
        check_vma=False,
    )
```

```python
import jax
import jax.numpy as jnp
from jax import lax
from jax.experimental import pallas as pl
from jax.experimental.pallas import tpu as pltpu
from jax.sharding import PartitionSpec as P

STAT_DECAY = 0.9


def over_core(value):
    size = lax.axis_size("rep")
    both = lax.all_gather(
        value, "rep", axis_index_groups=[[r, r + 1] for r in range(0, size, 2)]
    )
    return taken(both, 1 - lax.axis_index("rep") % 2)


def exchanged(value, mask):
    size = lax.axis_size("rep")
    return lax.ppermute(value, "rep", [(r, r ^ mask) for r in range(size)])


def passed(value, step):
    size = lax.axis_size("rep")
    return lax.ppermute(value, "rep", [(r, (r + step) % size) for r in range(size)])


def taken(value, index):
    return lax.dynamic_index_in_dim(value, index, 0, keepdims=False)


def either(first, own, other):
    return jnp.where(first, own, other), jnp.where(first, other, own)


def finish_kernel(
    core_ref, far_place_ref, own_place_ref,
    near_ref, far_ref, right_ref, left_ref, blank_ref,
    own_ref, given_ref, middle_ref,
):
    f32 = jnp.float32

    @pl.when(pl.program_id(0) == 0)
    def _():
        last = jnp.dot(far_ref[...], right_ref[0], preferred_element_type=f32)
        middle_ref[...] = (near_ref[...] + last).astype(middle_ref.dtype)

    result = jnp.dot(left_ref[0, 0], middle_ref[...], preferred_element_type=f32)
    sources, half, wide = given_ref.shape
    slab = wide // 2
    low = lax.broadcasted_iota(jnp.int32, (half, wide), 1) < slab
    for i in range(sources):
        upper = result[2 * i * half : (2 * i + 1) * half]
        lower = result[(2 * i + 1) * half : (2 * i + 2) * half]
        zero = jnp.where(low, upper, pltpu.roll(lower, slab, 1)).astype(given_ref.dtype)
        one = jnp.where(low, pltpu.roll(upper, slab, 1), lower).astype(given_ref.dtype)

        @pl.when(core_ref[0] == 0)
        def _():
            own_ref[0, i] = zero
            given_ref[i] = one

        @pl.when(core_ref[0] != 0)
        def _():
            own_ref[0, i] = one
            given_ref[i] = zero


def finish(core, far_place, own_place, near, far, right, left, blank):
    block, wide = far.shape
    _, sources, half, _ = blank.shape
    steps = 4
    few = sources // steps
    return pl.pallas_call(
        finish_kernel,
        grid_spec=pltpu.PrefetchScalarGridSpec(
            num_scalar_prefetch=3,
            grid=(steps,),
            in_specs=[
                pl.BlockSpec((block, wide), lambda i, c, f, o: (0, 0)),
                pl.BlockSpec((block, wide), lambda i, c, f, o: (0, 0)),
                pl.BlockSpec((1, wide, wide), lambda i, c, f, o: (f[0], 0, 0)),
                pl.BlockSpec((1, 1, block // steps, block), lambda i, c, f, o: (0, c[0], i, 0)),
                pl.BlockSpec(memory_space=pl.ANY),
            ],
            out_specs=[
                pl.BlockSpec((1, few, half, wide), lambda i, c, f, o: (o[0], i, 0, 0)),
                pl.BlockSpec((few, half, wide), lambda i, c, f, o: (i, 0, 0)),
            ],
            scratch_shapes=[pltpu.VMEM((block, wide), far.dtype)],
        ),
        out_shape=[
            jax.ShapeDtypeStruct(blank.shape, blank.dtype),
            jax.ShapeDtypeStruct((sources, half, wide), far.dtype),
        ],
        input_output_aliases={7: 0},
        compiler_params=pltpu.CompilerParams(vmem_limit_bytes=24 * 2**20),
    )(core.reshape(1), far_place.reshape(1), own_place.reshape(1), near, far, right, left, blank)


def place_kernel(owner_ref, back_ref, out_ref):
    half = back_ref.shape[1]
    col_blocks, slab = out_ref.shape[1:]
    picked = jnp.stack(
        [back_ref[owner_ref[c]].astype(jnp.float32) for c in range(col_blocks)]
    )
    picked = jnp.swapaxes(picked, 0, 1)
    out_ref[:half] = picked[:, :, :slab].astype(out_ref.dtype)
    out_ref[half:] = picked[:, :, slab:].astype(out_ref.dtype)


def place(owner_of, came_back, col_blocks):
    _, half, wide = came_back.shape
    shape = (2 * half, col_blocks, wide // 2)
    return pl.pallas_call(
        place_kernel,
        grid_spec=pltpu.PrefetchScalarGridSpec(
            num_scalar_prefetch=1,
            grid=(1,),
            in_specs=[pl.BlockSpec(came_back.shape, lambda i, o: (0, 0, 0))],
            out_specs=pl.BlockSpec(shape, lambda i, o: (0, 0, 0)),
        ),
        out_shape=jax.ShapeDtypeStruct(shape, came_back.dtype),
        compiler_params=pltpu.CompilerParams(vmem_limit_bytes=16 * 2**20),
    )(owner_of.astype(jnp.int32), came_back)


def local(grad_parts, slot_block, stat_left, stat_right, root_left, root_right):
    bf16, f32 = jnp.bfloat16, jnp.float32
    shard_rows, col_blocks = grad_parts.shape[1:3]
    block = stat_left.shape[3]
    owners, slot_count = slot_block.shape
    slab = root_right.shape[3]
    wide = 2 * slab
    chips = block // wide
    sources = block // shard_rows
    bands = owners // sources
    half = shard_rows // 2
    shard = lax.axis_index("fsdp")
    member = lax.axis_index("rep")
    core, chip = member % 2, member // 2
    first = core == 0
    my_band = shard // sources

    block_column = slot_block - my_band * col_blocks
    in_band = (slot_block >= 0) & (block_column >= 0) & (block_column < col_blocks)
    sends = jnp.any(
        in_band[:, :, None] & (block_column[:, :, None] == jnp.arange(col_blocks)), axis=1
    )
    owner_of = jnp.argmax(sends, axis=0)
    held = taken(slot_block, shard)
    held_band = held // col_blocks
    spare_band = (jnp.max(held_band) + 1) % bands
    places = jnp.where(held >= 0, held_band, spare_band).astype(jnp.uint32)
    own_place, other_place = either(first, places[0], places[1])

    partial = grad_parts[0]
    kept = lax.dynamic_slice_in_dim(partial, core * half, half, 0)
    given = lax.dynamic_slice_in_dim(partial, (1 - core) * half, half, 0)
    pair = kept.astype(f32) + over_core(given).astype(f32)
    side = chip % 2
    kept = lax.dynamic_slice_in_dim(pair, side * wide, wide, 2)
    given = lax.dynamic_slice_in_dim(pair, (1 - side) * wide, wide, 2)
    gradient = (kept + exchanged(given.astype(bf16), 2).astype(f32)).astype(bf16)

    outgoing = jnp.einsum(
        "oc,rcj->orj", sends.astype(bf16), gradient, preferred_element_type=f32
    ).astype(bf16)
    arrived = lax.all_to_all(outgoing, "fsdp", split_axis=0, concat_axis=0, tiled=True)
    blank = jnp.full((owners, half, wide), own_place // jnp.uint32(bands), bf16)
    arrived, own_place, other_place, owner_of = lax.optimization_barrier(
        (arrived, own_place, other_place, owner_of)
    )
    banded = arrived.reshape(bands, sources, half, wide)
    own, other = taken(banded, own_place), taken(banded, other_place)

    upper, lower = either(first, own, over_core(other))
    piece = jnp.stack([upper, lower], axis=1).reshape(block, wide)
    right_pair = either(
        first, taken(root_right[0], core), over_core(taken(root_right[0], 1 - core))
    )
    right = jnp.concatenate(right_pair, axis=1).reshape(chips, wide, wide)

    up, down = [piece], [piece]
    for _ in range(chips // 2 - 1):
        up.append(passed(up[-1], 2))
        down.append(passed(down[-1], -2))
    far = passed(up[-1], 2)

    def part(away, columns):
        rows = taken(right, ((chip + away) % chips).astype(jnp.uint32))
        return jnp.dot(columns, rows, preferred_element_type=f32)

    near = part(0, piece)
    for away in range(1, chips // 2):
        near = near + (part(away, down[away]) + part(chips - away, up[away]))
        if away == 1:
            near, blank = lax.optimization_barrier((near, blank))

    blank = blank.reshape(bands, sources, half, wide)
    far_place = (chip + chips // 2) % chips
    returning, given = finish(
        core, far_place, own_place.astype(jnp.int32), near, far, right, root_left, blank
    )
    returning = lax.dynamic_update_index_in_dim(returning, over_core(given), other_place, 0)
    returning = returning.reshape(owners, half, wide)
    slabs = down + [far] + up[:0:-1]
    *slabs, returning = lax.optimization_barrier((*slabs, returning))
    came_back = lax.all_to_all(returning, "fsdp", split_axis=0, concat_axis=0, tiled=True)
    piece = slabs[0]
    whole = jnp.concatenate(slabs, axis=1)
    rows = lax.dynamic_slice_in_dim(whole, chip * wide, wide, 0)
    left_rows = jnp.einsum("ic,kc->ik", rows, whole, preferred_element_type=f32)
    right_rows = jnp.einsum("ki,kc->ic", piece, whole, preferred_element_type=f32)
    right_rows = lax.dynamic_slice_in_dim(
        jnp.concatenate([right_rows, right_rows], axis=1),
        (chips - chip) % chips * wide,
        block,
        1,
    )
    both = jnp.stack([left_rows, right_rows])
    own = lax.dynamic_slice_in_dim(both, core * slab, slab, 1)
    other = exchanged(lax.dynamic_slice_in_dim(both, (1 - core) * slab, slab, 1), 1)
    products = jnp.stack(either(first, own, other), axis=1)
    came_back, products = lax.optimization_barrier((came_back, products))
    new_left = STAT_DECAY * stat_left[0] + (1.0 - STAT_DECAY) * products[0]
    new_right = STAT_DECAY * stat_right[0] + (1.0 - STAT_DECAY) * products[1]
    precond = place(owner_of, came_back, col_blocks)
    return (new_left[None], new_right[None], precond)


def solution(mesh):
    placed = (
        P("rep", "fsdp", None, None),
        P(),
        P("fsdp", None, "rep", None),
        P("fsdp", None, "rep", None),
        P("fsdp", None, None, None),
        P("fsdp", None, None, "rep"),
    )
    return jax.shard_map(
        local,
        mesh=mesh,
        in_specs=placed,
        out_specs=(
            P("fsdp", None, "rep", None),
            P("fsdp", None, "rep", None),
            P("fsdp", None, "rep"),
        ),
        check_vma=False,
    )
```
